32 devices in a mesh: ctx: 8 (over y, x, core), heads: 4 (over z).
Axes of the slice: x: 2, y: 2, z: 4, core: 2. Of those that a mesh axis runs over, the one named last changes fastest.
Arguments:
- queries: bfloat16 [1024, 16384], P('ctx', 'heads'), may hold values from -40 to 40
- cache_keys: bfloat16 [2, 16384, 1024], P(None, 'ctx', 'heads'), may hold values from -10 to 10
- cache_values: bfloat16 [2, 16384, 1024], P(None, 'ctx', 'heads'), may hold values from -6 to 6
- bounds: int32 [2, 2], replicated, may hold values from 1 to 16384, as said below
- out_weight: bfloat16 [16384, 16384], P('heads', 'ctx'), may hold values from -0.046875 to 0.046875
- residual: bfloat16 [1024, 16384], P('heads', 'ctx'), may hold values from -3 to 3
Outputs:
- layer_out: bfloat16 [1024, 16384], P('heads', 'ctx')
The draws below stay inside these ranges and needn't reach their ends.
Inputs may be any that keep to these rules, and one draw needn't show every extreme that they name: bounds[p, 0] lies between 8192 and 15872; bounds[p, 1] - bounds[p, 0] lies between 1 and 512.
All inputs are finite; a program needn't handle non-finite values.
Results may differ from the reference program's by a relative error of at most 0.012.
Values may be sent and summed in bfloat16 or wider, within the bound.
No kernel may reach another device: no remote copies, remote signals or barrier semaphores. Data moves between devices by JAX's collectives and lax.ppermute only.
A program may use at most 64 MiB of HBM per device.

```python
import math
import jax
import jax.numpy as jnp
from jax import lax

H = 128
KV = 8
HD = 128
D = 16384
PROMPTS = 2
Q = 512
CTX = 16384
ROWS = 1024


def shared_keys(key):
    base = jax.random.fold_in(key, 11)
    return 2.5 * jnp.clip(jax.random.normal(base, (PROMPTS, CTX, KV * HD), jnp.float32), -4.0, 4.0)


def draw_cache_keys(key, part):
    keys_all = shared_keys(key)
    return keys_all.astype(jnp.bfloat16)


def draw_queries(key, part):
    noise = jnp.clip(jax.random.normal(jax.random.fold_in(key, 23), (PROMPTS * Q, H * HD), jnp.float32), -4.0, 4.0)
    return noise.astype(jnp.bfloat16)


def draw_bounds(key, part):
    first_key, second_key, third_key = jax.random.split(jax.random.fold_in(key, 37), 3)
    start_first = CTX - Q - jax.random.randint(first_key, (1,), 0, Q)
    start_rest = jax.random.randint(second_key, (PROMPTS - 1,), CTX // 2, CTX - Q + 1)
    starts = jnp.concatenate([start_first, start_rest]).astype(jnp.int32)
    lengths = starts + jax.random.randint(third_key, (PROMPTS,), 1, Q + 1).astype(jnp.int32)
    return jnp.stack([starts, lengths], axis=1).astype(jnp.int32)


def levels(stream_key, shape, shards, least, high):
    def one(position, parts):
        steps = jax.random.uniform(jax.random.fold_in(jax.random.fold_in(stream_key, 6), position), (parts,), jnp.float32, least / len(shards), high / len(shards))
        return jnp.repeat(jnp.exp(steps), shape[position] // parts).reshape((-1,) + (1,) * (len(shape) - position - 1))

    level = one(*shards[0])
    for cut in shards[1:]:
        level = level * one(*cut)
    return level


def bell_draw(own_key, shape, spread, most, cuts=(), kind=jnp.bfloat16):
    values = spread * jax.random.normal(own_key, shape, jnp.float32)
    if cuts:
        values = values * levels(own_key, shape, cuts, -0.22, 0.18)
    return jnp.clip(values, -most, most).astype(kind)


def setup_inputs(seed: int = 0) -> dict:
    streams_of = jax.random.split(jax.random.key(seed), 7)
    return {
        "queries": draw_queries(jax.random.fold_in(streams_of[6], 71), 0),
        "cache_keys": draw_cache_keys(jax.random.fold_in(streams_of[6], 71), 0),
        "cache_values": bell_draw(streams_of[2], (PROMPTS, CTX, KV * HD), 1.0, 6.0, ((1, 8), (2, 4))),
        "bounds": draw_bounds(jax.random.fold_in(streams_of[6], 71), 0),
        "out_weight": bell_draw(streams_of[4], (D, D), D ** -0.5, 0.046875, ((0, 4), (1, 8))),
        "residual": bell_draw(streams_of[5], (ROWS, D), 0.5, 3.0, ((0, 4), (1, 8))),
    }


NEG_FILL = -1e+30

def reference(queries, cache_keys, cache_values, bounds, out_weight, residual):
    groups = H // KV
    scaling = 1.0 / math.sqrt(HD)
    key_pos = jnp.arange(CTX, dtype=jnp.int32)
    blocks = []
    for prompt in range(PROMPTS):
        begin = bounds[prompt, 0]
        length = bounds[prompt, 1]
        query_pos = begin + jnp.arange(Q, dtype=jnp.int32)
        visible = (key_pos[None, :] <= query_pos[:, None]) & (key_pos[None, :] < length)
        prompt_q = queries[prompt * Q:(prompt + 1) * Q].reshape(Q, H, HD)
        prompt_k = cache_keys[prompt].reshape(CTX, KV, HD)
        prompt_v = cache_values[prompt].reshape(CTX, KV, HD)

        def one_head(head):
            query_head = lax.dynamic_index_in_dim(prompt_q, head, 1, False)
            key_head = lax.dynamic_index_in_dim(prompt_k, head // groups, 1, False)
            value_head = lax.dynamic_index_in_dim(prompt_v, head // groups, 1, False)
            scores = jnp.dot(query_head, key_head.T, preferred_element_type=jnp.float32) * scaling
            scores = jnp.where(visible, scores, NEG_FILL)
            row_max = lax.optimization_barrier(jnp.max(scores, axis=1, keepdims=True))
            weights = jnp.where(visible, jnp.exp(scores - row_max), 0.0)
            total = lax.optimization_barrier(jnp.sum(weights, axis=1, keepdims=True))
            mixed = jnp.dot(weights.astype(jnp.bfloat16), value_head, preferred_element_type=jnp.float32)
            return (mixed / total).astype(jnp.bfloat16)
        heads_out = lax.map(one_head, jnp.arange(H, dtype=jnp.int32))
        blocks.append(jnp.transpose(heads_out, (1, 0, 2)).reshape(Q, H * HD))
    attended = jnp.concatenate(blocks, axis=0)
    projected = jnp.dot(attended, out_weight, preferred_element_type=jnp.float32)
    return (residual.astype(jnp.float32) + projected).astype(jnp.bfloat16)
```

```python
import functools
import math

import jax
import jax.numpy as jnp
from jax import lax
from jax.experimental import pallas as pl
from jax.experimental.pallas import tpu as pltpu
from jax.sharding import PartitionSpec as P

HD = 128
GROUPS = 16
NEG_FILL = -1e30
PARTS = 4
VMEM_LIMIT = 50 * 2**20


def attend_kernel(info_ref, base_ref, q_ref, *refs, pieces, first, last, width, sets, rows, stride):
    kvs = refs[:pieces]
    refs = refs[pieces:]
    if not first:
        acc_in, max_in = refs[:2]
        refs = refs[2:]
    if last:
        o_ref = refs[0]
        refs = refs[1:]
    else:
        acc_out, max_out = refs[:2]
        refs = refs[2:]
    bufs, lim_ref = refs[:2], refs[2]
    total = sets * rows * GROUPS
    start, length, place, member, part = [info_ref[i] for i in range(5)]
    part = part + pl.program_id(0)
    span = kvs[0].shape[1]
    blocks = [(p, j) for p in range(pieces) for j in range(span // width)]

    def work(masked):
        query = q_ref[...].reshape(sets * rows, GROUPS * HD).astype(jnp.float32)
        query = query * (math.log2(math.e) / math.sqrt(HD))
        high = query.astype(jnp.bfloat16)
        low = (query - high.astype(jnp.float32)).astype(jnp.bfloat16)

        def stacked(t):
            return jnp.concatenate([t[:, h * HD : (h + 1) * HD] for h in range(GROUPS)], axis=0)

        query = jnp.concatenate([stacked(high), stacked(low)], axis=1)
        if masked:
            index = lax.rem(lax.broadcasted_iota(jnp.int32, (total, HD), 0), sets * rows)
            row_set = lax.bitwise_xor(lax.div(index, rows), place)
            row = row_set * stride + member + part * rows + lax.rem(index, rows)
            lim_ref[...] = jnp.minimum(start + row + 1, length)

        def score(block, s_ref, running):
            p, j = block
            keys = kvs[p][0, j * width : (j + 1) * width, :]
            s = lax.dot_general(
                query,
                jnp.concatenate([keys, keys], axis=1),
                (((1,), (1,)), ((), ())),
                preferred_element_type=jnp.float32,
            )
            if masked:
                limit = lim_ref[...] - (base_ref[p] + j * width)
                limit = jnp.concatenate([limit] * (width // HD), axis=1)
                s = jnp.where(lax.broadcasted_iota(jnp.int32, s.shape, 1) < limit, s, NEG_FILL)
            s_ref[...] = s
            return jnp.maximum(running, jnp.max(s, axis=1, keepdims=True))

        def mix(block, s_ref, before, now, acc):
            p, j = block
            values = kvs[p][1, j * width : (j + 1) * width, :]
            values = jnp.concatenate([values, jnp.ones_like(values)], axis=1)
            weights = jnp.exp2(s_ref[...] - now).astype(jnp.bfloat16)
            new = jnp.dot(weights, values, preferred_element_type=jnp.float32)
            return new if acc is None else acc * jnp.exp2(before - now) + new

        if first:
            before, acc = jnp.full((total, 1), NEG_FILL, jnp.float32), None
        else:
            before, acc = max_in[0][:, :1], acc_in[0]
        now = score(blocks[0], bufs[0], before)
        for n, block in enumerate(blocks):
            more = n + 1 < len(blocks)
            if more:
                after = score(blocks[n + 1], bufs[(n + 1) % 2], now)
            acc = mix(block, bufs[n % 2], before, now, acc)
            if more:
                before, now = now, after
        if last:
            out = (acc[:, :HD] / acc[:, HD:]).astype(o_ref.dtype)
            for h in range(GROUPS):
                block = out[h * sets * rows : (h + 1) * sets * rows]
                o_ref[:, :, h * HD : (h + 1) * HD] = block.reshape(sets, rows, HD)
        else:
            acc_out[0] = acc
            max_out[0] = jnp.broadcast_to(now, (total, HD))

    furthest = base_ref[0]
    for p in range(1, pieces):
        furthest = jnp.maximum(furthest, base_ref[p])
    whole = furthest + span <= jnp.minimum(start + 1, length)

    @pl.when(whole)
    def _():
        work(False)

    @pl.when(jnp.logical_not(whole))
    def _():
        work(True)


def attend(info, base, query, kvs, state, last, parts, stride):
    sets, all_rows, cols = query.shape
    rows = all_rows // parts
    total = sets * rows * GROUPS
    first = state is None
    span = kvs[0].shape[1]
    in_specs = [pl.BlockSpec((sets, rows, cols), lambda t, *_: (0, t, 0))]
    in_specs += [pl.BlockSpec(k.shape, lambda t, *_: (0, 0, 0)) for k in kvs]
    kept = [
        pl.BlockSpec((1, total, 2 * HD), lambda t, *_: (t, 0, 0)),
        pl.BlockSpec((1, total, HD), lambda t, *_: (t, 0, 0)),
    ]
    args = [query] + list(kvs)
    if not first:
        in_specs += kept
        args += list(state)
    if last:
        out_shape = jax.ShapeDtypeStruct((sets, all_rows, cols), jnp.bfloat16)
        out_specs = pl.BlockSpec((sets, rows, cols), lambda t, *_: (0, t, 0))
    else:
        out_shape = (
            jax.ShapeDtypeStruct((parts, total, 2 * HD), jnp.float32),
            jax.ShapeDtypeStruct((parts, total, HD), jnp.float32),
        )
        out_specs = tuple(kept)
    width = min(1024, span)
    positions = span * len(kvs)
    return pl.pallas_call(
        functools.partial(
            attend_kernel,
            pieces=len(kvs),
            first=first,
            last=last,
            width=width,
            sets=sets,
            rows=rows,
            stride=stride,
        ),
        out_shape=out_shape,
        grid_spec=pltpu.PrefetchScalarGridSpec(
            num_scalar_prefetch=2,
            grid=(parts,),
            in_specs=in_specs,
            out_specs=out_specs,
            scratch_shapes=[pltpu.VMEM((total, width), jnp.float32)] * 2
            + [pltpu.VMEM((total, HD), jnp.int32)],
        ),
        cost_estimate=pl.CostEstimate(
            flops=parts * total * positions * HD * 10,
            bytes_accessed=positions * HD * 4 + parts * total * HD * 4,
            transcendentals=parts * total * positions,
        ),
        compiler_params=pltpu.CompilerParams(vmem_limit_bytes=VMEM_LIMIT),
    )(info, base, *args)


def project_kernel(where_ref, *refs, pieces, sets):
    ins, w_ref, o_ref, lhs = refs[:pieces], refs[pieces], refs[pieces + 1], refs[pieces + 2]

    @pl.when(pl.program_id(0) == 0)
    def _():
        for i, ref in enumerate(ins):
            column = where_ref[2 * i]
            for s in range(sets):
                lhs[column, where_ref[2 * i + 1] + lax.bitwise_xor(s, column) * where_ref[2 * pieces]] = ref[s]

    cols = lhs.shape[3]
    acc = None
    for c in range(lhs.shape[0]):
        left = lhs[c].reshape(lhs.shape[1] * lhs.shape[2], cols)
        term = jnp.dot(left, w_ref[c * cols : (c + 1) * cols, :], preferred_element_type=jnp.float32)
        acc = term if acc is None else acc + term
    o_ref[...] = acc.astype(o_ref.dtype)


def project(where, pieces, weight, devices):
    sets, rows, cols = pieces[0].shape
    depth, out_cols = weight.shape
    width = min(512, out_cols)
    total = devices * rows
    return pl.pallas_call(
        functools.partial(project_kernel, pieces=len(pieces), sets=sets),
        out_shape=jax.ShapeDtypeStruct((total, out_cols), jnp.bfloat16),
        grid_spec=pltpu.PrefetchScalarGridSpec(
            num_scalar_prefetch=1,
            grid=(out_cols // width,),
            in_specs=[pl.BlockSpec(p.shape, lambda t, *_: (0, 0, 0)) for p in pieces]
            + [pl.BlockSpec((depth, width), lambda t, *_: (0, t))],
            out_specs=pl.BlockSpec((total, width), lambda t, *_: (0, t)),
            scratch_shapes=[pltpu.VMEM((depth // cols, devices, rows, cols), jnp.bfloat16)],
        ),
        cost_estimate=pl.CostEstimate(
            flops=2 * total * depth * out_cols,
            bytes_accessed=2 * (depth * out_cols + total * out_cols + total * depth),
            transcendentals=0,
        ),
        compiler_params=pltpu.CompilerParams(vmem_limit_bytes=VMEM_LIMIT),
    )(where, *pieces, weight)


def crossed(block, bits):
    count = lax.axis_size("ctx")
    return lax.ppermute(block, "ctx", [(i, i ^ bits) for i in range(count)])


def scatter_sum(own, residual):
    size = lax.axis_size("heads")
    here = lax.axis_index("heads")
    blocks = own.reshape(size, own.shape[0] // size, own.shape[1])

    def mine(index):
        return lax.dynamic_index_in_dim(blocks, jnp.clip(index, 0, size - 1), 0, False).astype(jnp.float32)

    up = down = None
    for step in range(1, size):
        send_up, send_down = mine(size + here - step), mine(here - size + step)
        if step > 1:
            send_up, send_down = send_up + up, send_down + down
        up = lax.ppermute(send_up.astype(jnp.bfloat16), "heads", [(z, z + 1) for z in range(min(step, size - 1))])
        down = lax.ppermute(
            send_down.astype(jnp.bfloat16), "heads", [(size - 1 - z, size - 2 - z) for z in range(min(step, size - 1))]
        )
        up, down = up.astype(jnp.float32), down.astype(jnp.float32)
    total = residual.astype(jnp.float32) + (mine(here) + up + down)
    return total.astype(jnp.bfloat16)


def shards(queries, cache_keys, cache_values, bounds, out_weight, residual):
    rows = queries.shape[0]
    prompts, span, _ = cache_keys.shape
    local_kv = cache_keys.shape[2] // HD
    cols = GROUPS * HD
    devices = lax.axis_size("ctx")
    position = lax.axis_index("ctx")
    jobs = prompts * local_kv
    members = devices // jobs
    job, member = position // members, position % members
    prompt, place = job // local_kv, job % local_kv
    parts = PARTS

    def query_for(kv):
        return lax.dynamic_slice_in_dim(queries, kv * cols, cols, 1)

    def cache_for(j):
        where = (j // local_kv, 0, (j % local_kv) * HD)
        return jnp.concatenate(
            [lax.dynamic_slice(t, where, (1, span, HD)) for t in (cache_keys, cache_values)], axis=0
        )

    query = jnp.stack(
        [query_for(place)] + [crossed(query_for(place ^ k), k * members) for k in range(1, local_kv)]
    )
    order = [0] + sorted(range(1, jobs), key=lambda k: (k < local_kv, k) if k != jobs - 1 else (2, k))
    arrived = {}
    for k in order:
        block = cache_for(job ^ k)
        arrived[k] = [crossed(block, k * members) if k else block]
        arrived[k] += [crossed(arrived[k][0], m) for m in range(1, members)]

    def bases(ks):
        return jnp.stack([((job ^ k) * members + (member ^ m)) * span for k in ks for m in range(members)])

    limits = lax.dynamic_index_in_dim(bounds, prompt, 0, False)

    def info(part):
        return jnp.stack([limits[0], limits[1], place, member * rows, jnp.int32(part)]).astype(jnp.int32)

    stride = members * rows
    state = None
    early = order[: len(order) // 2]
    late = order[len(order) // 2 :]
    for k in early:
        state = attend(info(0), bases([k]), query, arrived[k], state, False, parts, stride)
    where = []
    for k in range(jobs):
        for m in range(members):
            source = job ^ k
            where += [source % local_kv, (source // local_kv) * local_kv * members + (member ^ m)]
    where = jnp.stack(where + [jnp.int32(members)]).astype(jnp.int32)

    here_rows = residual.shape[0]
    size = lax.axis_size("heads")
    step = rows // parts
    blocks = residual.reshape(devices // size, rows, residual.shape[1])
    outs = []
    for part in range(parts):
        piece = attend(
            info(part),
            bases(late),
            query[:, part * step : (part + 1) * step],
            [t for k in late for t in arrived[k]],
            tuple(t[part : part + 1] for t in state),
            True,
            1,
            stride,
        )
        got = [piece] + [crossed(piece, k * members) for k in range(1, jobs)]
        pieces = []
        for t in got:
            pieces += [t] + [crossed(t, m) for m in range(1, members)]
        partial = project(where, pieces, out_weight, devices)
        res = blocks[:, part * step : (part + 1) * step].reshape(-1, residual.shape[1])
        outs.append(scatter_sum(partial, res).reshape(devices // size, step, residual.shape[1]))
    return jnp.concatenate(outs, axis=1).reshape(here_rows, residual.shape[1])


def solution(mesh):
    in_specs = (
        P("ctx", "heads"),
        P(None, "ctx", "heads"),
        P(None, "ctx", "heads"),
        P(),
        P("heads", "ctx"),
        P("heads", "ctx"),
    )
    out_specs = P("heads", "ctx")
    return jax.shard_map(shards, mesh=mesh, in_specs=in_specs, out_specs=out_specs, check_vma=False)
```

```python
import functools
import math

import jax
import jax.numpy as jnp
from jax import lax
from jax.experimental import pallas as pl
from jax.experimental.pallas import tpu as pltpu
from jax.sharding import PartitionSpec as P

HD = 128
GROUPS = 16
COLS = GROUPS * HD
NEG_FILL = -1e30
PARTS = 4
VMEM_LIMIT = 50 * 2**20


def pack_kernel(q_ref, k_ref, v_ref, *refs, jobs_of, kvs_of, members, local_kv):
    outs, sems = refs[:-1], refs[-1]
    job = lax.div(lax.axis_index("ctx"), members)
    copies = []
    for out, k in zip(outs, jobs_of, strict=False):
        other = lax.bitwise_xor(job, k)
        prompt, place = lax.div(other, local_kv), lax.rem(other, local_kv)
        for i, ref in enumerate((k_ref, v_ref)):
            copies.append((ref.at[prompt, :, pl.ds(pl.multiple_of(place * HD, HD), HD)], out.at[i]))
    for out, k in zip(outs[len(jobs_of) :], kvs_of, strict=True):
        place = lax.rem(lax.bitwise_xor(job, k), local_kv)
        copies.append((q_ref.at[:, pl.ds(pl.multiple_of(place * COLS, COLS), COLS)], out))
    copies = [pltpu.make_async_copy(a, b, sems.at[n]) for n, (a, b) in enumerate(copies)]
    for c in copies:
        c.start()
    for c in copies:
        c.wait()


def pack(queries, keys, values, jobs_of, kvs_of, members, local_kv):
    slab = jax.ShapeDtypeStruct((2, keys.shape[1], HD), keys.dtype)
    cut = jax.ShapeDtypeStruct((queries.shape[0], COLS), queries.dtype)
    anywhere = pl.BlockSpec(memory_space=pl.ANY)
    outs = [slab] * len(jobs_of) + [cut] * len(kvs_of)
    return pl.pallas_call(
        functools.partial(pack_kernel, jobs_of=jobs_of, kvs_of=kvs_of, members=members, local_kv=local_kv),
        out_shape=outs,
        in_specs=[anywhere] * 3,
        out_specs=[pl.BlockSpec(memory_space=pltpu.VMEM)] * len(outs),
        scratch_shapes=[pltpu.SemaphoreType.DMA((2 * len(jobs_of) + len(kvs_of),))],
        compiler_params=pltpu.CompilerParams(vmem_limit_bytes=VMEM_LIMIT),
        cost_estimate=pl.CostEstimate(flops=0, bytes_accessed=sum(2 * 2 * math.prod(o.shape) for o in outs), transcendentals=0),
    )(queries, keys, values)


def attend_kernel(part_ref, bounds_ref, *refs, labels, sets, first, last, width, rows, members, local_kv):
    queries, kvs = refs[:sets], refs[sets : sets + len(labels)]
    refs = refs[sets + len(labels) :]
    if not first:
        state_in, refs = refs[0], refs[1:]
    out_ref, buf_a, buf_b, lim_ref = refs
    bufs = (buf_a, buf_b)
    position = lax.axis_index("ctx")
    job, member = lax.div(position, members), lax.rem(position, members)
    prompt, place = lax.div(job, local_kv), lax.rem(job, local_kv)
    start, length = bounds_ref[prompt, 0], bounds_ref[prompt, 1]
    part = part_ref[0] + pl.program_id(0)
    total = sets * rows * GROUPS
    span = kvs[0].shape[1]
    bases = [(lax.bitwise_xor(job, k) * members + lax.bitwise_xor(member, m)) * span for k, m in labels]
    blocks = [(p, j) for p in range(len(labels)) for j in range(span // width)]

    query = jnp.concatenate([q[...] for q in queries], axis=0).astype(jnp.float32)
    query = query * (math.log2(math.e) / math.sqrt(HD))
    high = query.astype(jnp.bfloat16)
    low = (query - high.astype(jnp.float32)).astype(jnp.bfloat16)

    def stacked(t):
        return jnp.concatenate([t[:, h * HD : (h + 1) * HD] for h in range(GROUPS)], axis=0)

    query = jnp.concatenate([stacked(high), stacked(low)], axis=1)
    clear = jnp.minimum(start + 1, length)
    furthest = bases[0]
    for b in bases[1:]:
        furthest = jnp.maximum(furthest, b)

    def set_limits():
        index = lax.rem(lax.broadcasted_iota(jnp.int32, (total, HD), 0), sets * rows)
        row_set = lax.bitwise_xor(lax.div(index, rows), place)
        row = (row_set * members + member) * (rows * PARTS) + part * rows + lax.rem(index, rows)
        lim_ref[...] = jnp.minimum(start + row + 1, length)

    def score(block, s_ref, running, masked):
        p, j = block
        masked = p in masked
        keys = kvs[p][0, j * width : (j + 1) * width, :]
        s = lax.dot_general(
            query,
            jnp.concatenate([keys, keys], axis=1),
            (((1,), (1,)), ((), ())),
            preferred_element_type=jnp.float32,
        )
        if masked:
            limit = jnp.concatenate([lim_ref[...] - (bases[p] + j * width)] * (width // HD), axis=1)
            s = jnp.where(lax.broadcasted_iota(jnp.int32, s.shape, 1) < limit, s, NEG_FILL)
        s_ref[...] = s
        return jnp.maximum(running, jnp.max(s, axis=1, keepdims=True))

    def mix(block, s_ref, before, now, acc):
        p, j = block
        values = kvs[p][1, j * width : (j + 1) * width, :]
        values = jnp.concatenate([values, jnp.ones_like(values)], axis=1)
        weights = jnp.exp2(s_ref[...] - now).astype(jnp.bfloat16)
        new = jnp.dot(weights, values, preferred_element_type=jnp.float32)
        return new if acc is None else acc * jnp.exp2(before - now) + new

    def work(masked):
        if masked:
            set_limits()
        if first:
            before, acc = jnp.full((total, 1), NEG_FILL, jnp.float32), None
        else:
            kept = state_in[0]
            before = kept[:, HD : HD + 1]
            acc = jnp.concatenate([kept[:, :HD], jnp.broadcast_to(kept[:, 2 * HD - 1 :], (total, HD))], axis=1)
        now = score(blocks[0], bufs[0], before, masked)
        for n, block in enumerate(blocks):
            more = n + 1 < len(blocks)
            if more:
                after = score(blocks[n + 1], bufs[(n + 1) % 2], now, masked)
            acc = mix(block, bufs[n % 2], before, now, acc)
            if more:
                before, now = now, after
        if last:
            out = (acc[:, :HD] / acc[:, HD:]).astype(out_ref.dtype)
            for h in range(GROUPS):
                block = out[h * sets * rows : (h + 1) * sets * rows]
                out_ref[:, :, h * HD : (h + 1) * HD] = block.reshape(sets, rows, HD)
        else:
            lane = lax.broadcasted_iota(jnp.int32, (total, HD), 1)
            out_ref[0, :, :HD] = acc[:, :HD]
            out_ref[0, :, HD:] = jnp.where(lane < HD // 2, jnp.broadcast_to(now, (total, HD)), acc[:, HD:])

    everything = frozenset(range(len(labels)))
    if first:

        @pl.when(furthest + span <= clear)
        def _():
            work(frozenset())

        @pl.when(furthest + span > clear)
        def _():
            work(everything)
    elif last:
        work(everything)
    else:
        jobs = lax.axis_size("ctx") // members
        second_half = job >= jobs // 2
        near = frozenset(p for p, (k, _) in enumerate(labels) if k < jobs // 2)

        @pl.when(second_half)
        def _():
            work(near)

        @pl.when(jnp.logical_not(second_half))
        def _():
            work(everything - near)


def attend(part, bounds, queries, kvs, labels, state, last, count, members):
    sets = len(queries)
    rows = queries[0].shape[0] // PARTS
    total = sets * rows * GROUPS
    span = kvs[0].shape[1]
    in_specs = [pl.BlockSpec((rows, COLS), lambda t, part, _: (part[0] + t, 0))] * sets
    in_specs += [pl.BlockSpec(k.shape, lambda t, *_: (0, 0, 0)) for k in kvs]
    kept = pl.BlockSpec((1, total, 2 * HD), lambda t, part, _: (part[0] + t, 0, 0))
    args = list(queries) + list(kvs)
    if state is not None:
        in_specs += [kept]
        args += [state]
    if last:
        out_shape = jax.ShapeDtypeStruct((sets, count * rows, COLS), jnp.bfloat16)
        out_spec = pl.BlockSpec((sets, rows, COLS), lambda t, *_: (0, t, 0))
    else:
        out_shape = jax.ShapeDtypeStruct((count, total, 2 * HD), jnp.float32)
        out_spec = kept
    width = min(1024, span)
    positions = span * len(kvs)
    return pl.pallas_call(
        functools.partial(
            attend_kernel,
            labels=labels,
            sets=sets,
            first=state is None,
            last=last,
            width=width,
            rows=rows,
            members=members,
            local_kv=sets,
        ),
        out_shape=out_shape,
        grid_spec=pltpu.PrefetchScalarGridSpec(
            num_scalar_prefetch=2,
            grid=(count,),
            in_specs=in_specs,
            out_specs=out_spec,
            scratch_shapes=[pltpu.VMEM((total, width), jnp.float32)] * 2 + [pltpu.VMEM((total, HD), jnp.int32)],
        ),
        cost_estimate=pl.CostEstimate(
            flops=count * total * positions * HD * 10,
            bytes_accessed=positions * HD * 4 + count * total * HD * 4,
            transcendentals=count * total * positions,
        ),
        compiler_params=pltpu.CompilerParams(vmem_limit_bytes=VMEM_LIMIT),
    )(jnp.full((1,), part, jnp.int32), bounds, *args)


def project_kernel(*refs, members, local_kv, size, devices):
    ins, (w_ref, keep_ref, send_ref, lhs) = refs[:members], refs[members:]

    @pl.when(pl.program_id(0) == 0)
    def _():
        position, here = lax.axis_index("ctx"), lax.axis_index("heads")
        job, member = lax.div(position, members), lax.rem(position, members)
        share = devices // size
        for m, ref in enumerate(ins):
            for k in range(ref.shape[0]):
                source = lax.bitwise_xor(job, k)
                column = lax.rem(source, local_kv)
                for s in range(local_kv):
                    row_set = lax.bitwise_xor(s, column)
                    owner = (source - column + row_set) * members + lax.bitwise_xor(member, m)
                    away, slot = lax.bitwise_xor(lax.div(owner, share), here), 0
                    bits = size.bit_length() - 1
                    for b in range(bits):
                        slot = slot + lax.rem(lax.div(away, 2**b), 2) * 2 ** (bits - 1 - b)
                    lhs[column, slot * share + lax.rem(owner, share)] = ref[k, s]

    rows, cols = lhs.shape[1] * lhs.shape[2], lhs.shape[3]
    acc = None
    for c in range(lhs.shape[0]):
        left = lhs[c].reshape(rows, cols)
        term = jnp.dot(left, w_ref[c * cols : (c + 1) * cols, :], preferred_element_type=jnp.float32)
        acc = term if acc is None else acc + term
    keep_ref[...] = acc[: rows // 2].astype(keep_ref.dtype)
    send_ref[...] = acc[rows // 2 :].astype(send_ref.dtype)


def project(pieces, weight, devices, size):
    jobs, sets, rows, cols = pieces[0].shape
    depth, out_cols = weight.shape
    width = min(512, out_cols)
    total = devices * rows
    half = jax.ShapeDtypeStruct((total // 2, out_cols), jnp.bfloat16)
    return pl.pallas_call(
        functools.partial(
            project_kernel, members=len(pieces), local_kv=sets, size=size, devices=devices
        ),
        out_shape=(half, half),
        grid=(out_cols // width,),
        in_specs=[pl.BlockSpec(p.shape, lambda t: (0, 0, 0, 0)) for p in pieces]
        + [pl.BlockSpec((depth, width), lambda t: (0, t))],
        out_specs=(pl.BlockSpec((total // 2, width), lambda t: (0, t)),) * 2,
        scratch_shapes=[pltpu.VMEM((sets, devices, rows, cols), jnp.bfloat16)],
        cost_estimate=pl.CostEstimate(
            flops=2 * total * depth * out_cols,
            bytes_accessed=2 * (depth * out_cols + total * out_cols + total * depth),
            transcendentals=0,
        ),
        compiler_params=pltpu.CompilerParams(vmem_limit_bytes=VMEM_LIMIT),
    )(*pieces, weight)


def crossed(block, bits, axis="ctx"):
    return lax.ppermute(block, axis, [(i, i ^ bits) for i in range(lax.axis_size(axis))])


def after(block, *others):
    return lax.optimization_barrier((block,) + others)[0]


def shards(queries, cache_keys, cache_values, bounds, out_weight, residual):
    rows = queries.shape[0]
    prompts = cache_keys.shape[0]
    local_kv = cache_keys.shape[2] // HD
    devices, size = lax.axis_size("ctx"), lax.axis_size("heads")
    jobs = prompts * local_kv
    members = devices // jobs
    every = range(1, members)
    final = jobs - 1
    middle = list(range(jobs - 2, 0, -1))
    kvs_of = list(range(local_kv))

    ready = pack(queries, cache_keys, cache_values, middle[:1] + [0], kvs_of, members, local_kv)
    slabs = dict(zip(middle[:1] + [0], ready, strict=False))
    queries_of = ready[len(slabs) :]
    rest = middle[1:] + [final]
    slabs.update(zip(rest, pack(after(queries, ready[0]), cache_keys, cache_values, rest, [], members, local_kv), strict=True))

    query = [queries_of[0]] + [crossed(queries_of[k], k * members) for k in range(1, local_kv)]
    got = {(0, 0): slabs[0]}
    for k in middle + [final]:
        got[k, 0] = crossed(slabs[k], k * members)
    for m in every:
        got[0, m] = crossed(got[0, 0], m)
    labels = [(0, m) for m in range(members)]
    state = attend(0, bounds, query, [got[i] for i in labels], labels, None, False, PARTS, members)
    if middle:
        direct = [(k, 0) for k in middle]
        for i in direct:
            got[i] = after(got[i], state)
        for k in middle:
            for m in every:
                got[k, m] = crossed(got[k, 0], m)
        state = attend(0, bounds, query, [got[i] for i in direct], direct, state, False, PARTS, members)
    got[final, 0] = after(got[final, 0], state)
    for m in every:
        got[final, m] = crossed(got[final, 0], m)
    labels = [(k, m) for k in middle for m in every] + [(final, m) for m in range(members)]

    step = rows // PARTS
    blocks = residual.reshape(devices // size, rows, residual.shape[1])
    pieces, packs, partials, sums, outs = {}, {}, {}, {}, {}

    def late(part, *waits):
        q = [after(query[0], *waits)] + query[1:] if waits else query
        pieces[part] = attend(part, bounds, q, [got[i] for i in labels], labels, state, True, 1, members)

    def gathered(part, *waits):
        received = [crossed(pieces[part], k * members) for k in range(1, jobs)]
        if part + 1 in pieces:
            received = list(after(tuple(received), pieces[part + 1]))
        own = jnp.stack([pieces[part]] + received)
        packs[part] = [own] + [crossed(own, m) for m in every]

    def projected(part, *waits):
        own = after(packs[part][0], *waits) if waits else packs[part][0]
        partials[part] = project([own] + packs[part][1:], out_weight, devices, size)

    def sent(part, level):
        return crossed((partials[part] if level == 0 else sums[part])[1], 2**level, "heads")

    def combined(part, level, got):
        keep = (partials[part] if level == 0 else sums[part])[0].astype(jnp.float32)
        got = got.astype(jnp.float32)
        if 2 ** (level + 1) < size:
            half = keep.shape[0] // 2
            sums[part] = keep[:half] + got[:half], (keep[half:] + got[half:]).astype(jnp.bfloat16)
        else:
            res = blocks[:, part * step : (part + 1) * step].reshape(-1, residual.shape[1])
            total = res.astype(jnp.float32) + (keep + got)
            outs[part] = total.astype(jnp.bfloat16).reshape(devices // size, step, residual.shape[1])

    levels = size.bit_length() - 1
    for turn in range(PARTS + 1 + levels):
        if turn < PARTS:
            waits = [pieces[turn - 1]] if turn >= 1 else []
            if turn >= 2:
                waits.append(partials[turn - 2][0])
            late(turn, *waits)
        if turn == PARTS:
            gathered(turn - 1)
        here = [(turn - 2 - level, level) for level in range(levels) if 0 <= turn - 2 - level < PARTS]
        received = [sent(part, level) for part, level in here]
        if received and turn < PARTS:
            received, pieces[turn] = after((received, pieces[turn]))
        elif received and turn == PARTS:
            received = after(received, packs[turn - 1][0])
        for (part, level), block in zip(here, received, strict=True):
            combined(part, level, block)
        part = turn - 1
        if 0 <= part < PARTS:
            if turn < PARTS:
                gathered(part)
            waits = [sums[part - 1][1]] if part - 1 in sums and turn < PARTS else []
            projected(part, *waits)
    return jnp.concatenate([outs[p] for p in range(PARTS)], axis=1).reshape(residual.shape)


def solution(mesh):
    in_specs = (
        P("ctx", "heads"),
        P(None, "ctx", "heads"),
        P(None, "ctx", "heads"),
        P(),
        P("heads", "ctx"),
        P("heads", "ctx"),
    )
    out_specs = P("heads", "ctx")
    return jax.shard_map(shards, mesh=mesh, in_specs=in_specs, out_specs=out_specs, check_vma=False)
```

```python
import functools
import math

import jax
import jax.numpy as jnp
from jax import lax
from jax.experimental import pallas as pl
from jax.experimental.pallas import tpu as pltpu
from jax.sharding import PartitionSpec as P

HD = 128
GROUPS = 16
COLS = GROUPS * HD
NEG_FILL = -1e30
PARTS = 4
CUTS = 2
VMEM_LIMIT = 50 * 2**20


def pack_kernel(q_ref, k_ref, v_ref, *refs, jobs_of, kvs_of, members, local_kv):
    outs, sems = refs[:-1], refs[-1]
    job = lax.div(lax.axis_index("ctx"), members)
    copies = []
    for out, k in zip(outs, jobs_of, strict=False):
        other = lax.bitwise_xor(job, k)
        prompt, place = lax.div(other, local_kv), lax.rem(other, local_kv)
        for i, ref in enumerate((k_ref, v_ref)):
            copies.append((ref.at[prompt, :, pl.ds(pl.multiple_of(place * HD, HD), HD)], out.at[i]))
    for out, k in zip(outs[len(jobs_of) :], kvs_of, strict=True):
        place = lax.rem(lax.bitwise_xor(job, k), local_kv)
        copies.append((q_ref.at[:, pl.ds(pl.multiple_of(place * COLS, COLS), COLS)], out))
    copies = [pltpu.make_async_copy(a, b, sems.at[n]) for n, (a, b) in enumerate(copies)]
    for c in copies:
        c.start()
    for c in copies:
        c.wait()


def pack(queries, keys, values, jobs_of, kvs_of, members, local_kv):
    slab = jax.ShapeDtypeStruct((2, keys.shape[1], HD), keys.dtype)
    cut = jax.ShapeDtypeStruct((queries.shape[0], COLS), queries.dtype)
    anywhere = pl.BlockSpec(memory_space=pl.ANY)
    outs = [slab] * len(jobs_of) + [cut] * len(kvs_of)
    return pl.pallas_call(
        functools.partial(pack_kernel, jobs_of=jobs_of, kvs_of=kvs_of, members=members, local_kv=local_kv),
        out_shape=outs,
        in_specs=[anywhere] * 3,
        out_specs=[pl.BlockSpec(memory_space=pltpu.VMEM)] * len(outs),
        scratch_shapes=[pltpu.SemaphoreType.DMA((2 * len(jobs_of) + len(kvs_of),))],
        compiler_params=pltpu.CompilerParams(vmem_limit_bytes=VMEM_LIMIT),
        cost_estimate=pl.CostEstimate(flops=0, bytes_accessed=sum(2 * 2 * math.prod(o.shape) for o in outs), transcendentals=0),
    )(queries, keys, values)


def attend_kernel(part_ref, bounds_ref, *refs, labels, sets, subs, first, last, width, rows, members, local_kv):
    queries, kvs = refs[: len(sets)], refs[len(sets) : len(sets) + len(labels)]
    refs = refs[len(sets) + len(labels) :]
    if not first:
        states_in, refs = refs[: len(sets)], refs[len(sets) :]
    outs, (buf_a, buf_b, lim_ref) = refs[:-3], refs[-3:]
    bufs = (buf_a, buf_b)
    position = lax.axis_index("ctx")
    job, member = lax.div(position, members), lax.rem(position, members)
    prompt, place = lax.div(job, local_kv), lax.rem(job, local_kv)
    start, length = bounds_ref[prompt, 0], bounds_ref[prompt, 1]
    part = part_ref[0] + pl.program_id(0) * subs
    unit = rows * GROUPS
    total = len(sets) * subs * unit
    span = kvs[0].shape[1]
    bases = [(lax.bitwise_xor(job, k) * members + lax.bitwise_xor(member, m)) * span for k, m in labels]
    blocks = [(p, j) for p in range(len(labels)) for j in range(span // width)]

    query = jnp.concatenate([q[...] for q in queries], axis=0).astype(jnp.float32)
    query = query * (math.log2(math.e) / math.sqrt(HD))
    high = query.astype(jnp.bfloat16)
    low = (query - high.astype(jnp.float32)).astype(jnp.bfloat16)

    def stacked(t):
        parts = range(0, len(sets) * subs * rows, rows)
        return jnp.concatenate([t[n : n + rows, h * HD : (h + 1) * HD] for n in parts for h in range(GROUPS)], axis=0)

    query = jnp.concatenate([stacked(high), stacked(low)], axis=1)
    clear = jnp.minimum(start + 1, length)
    furthest = bases[0]
    for b in bases[1:]:
        furthest = jnp.maximum(furthest, b)

    def set_limits():
        index = lax.broadcasted_iota(jnp.int32, (total, HD), 0)
        which = lax.div(index, unit)
        row_set = lax.bitwise_xor(lax.div(which, subs) + sets[0], place)
        row = (part + lax.rem(which, subs)) * rows + lax.rem(index, rows)
        row = row + (row_set * members + member) * (rows * PARTS)
        lim_ref[...] = jnp.minimum(start + row + 1, length)

    def score(block, s_ref, running, masked):
        p, j = block
        masked = p in masked
        keys = kvs[p][0, j * width : (j + 1) * width, :]
        s = lax.dot_general(
            query,
            jnp.concatenate([keys, keys], axis=1),
            (((1,), (1,)), ((), ())),
            preferred_element_type=jnp.float32,
        )
        if masked:
            limit = jnp.concatenate([lim_ref[...] - (bases[p] + j * width)] * (width // HD), axis=1)
            s = jnp.where(lax.broadcasted_iota(jnp.int32, s.shape, 1) < limit, s, NEG_FILL)
        s_ref[...] = s
        return jnp.maximum(running, jnp.max(s, axis=1, keepdims=True))

    def mix(block, s_ref, before, now, acc):
        p, j = block
        values = kvs[p][1, j * width : (j + 1) * width, :]
        values = jnp.concatenate([values, jnp.ones_like(values)], axis=1)
        weights = jnp.exp2(s_ref[...] - now).astype(jnp.bfloat16)
        new = jnp.dot(weights, values, preferred_element_type=jnp.float32)
        return new if acc is None else acc * jnp.exp2(before - now) + new

    def work(masked):
        if masked:
            set_limits()
        if first:
            before, acc = jnp.full((total, 1), NEG_FILL, jnp.float32), None
        else:
            kept = jnp.concatenate([t[...].reshape(subs * unit, 2 * HD) for t in states_in], axis=0)
            before = kept[:, HD : HD + 1]
            acc = jnp.concatenate([kept[:, :HD], jnp.broadcast_to(kept[:, 2 * HD - 1 :], (total, HD))], axis=1)
        now = score(blocks[0], bufs[0], before, masked)
        for n, block in enumerate(blocks):
            more = n + 1 < len(blocks)
            if more:
                after = score(blocks[n + 1], bufs[(n + 1) % 2], now, masked)
            acc = mix(block, bufs[n % 2], before, now, acc)
            if more:
                before, now = now, after
        if last:
            out = (acc[:, :HD] / acc[:, HD:]).astype(outs[0].dtype)
            for n in range(len(sets)):
                for h in range(GROUPS):
                    begin = n * unit + h * rows
                    outs[0][n, :, h * HD : (h + 1) * HD] = out[begin : begin + rows]
        else:
            lane = lax.broadcasted_iota(jnp.int32, (total, HD), 1)
            stats = jnp.where(lane < HD // 2, jnp.broadcast_to(now, (total, HD)), acc[:, HD:])
            for n, out_ref in enumerate(outs):
                rest = slice(n * subs * unit, (n + 1) * subs * unit)
                out_ref[:, :, :HD] = acc[rest, :HD].reshape(subs, unit, HD)
                out_ref[:, :, HD:] = stats[rest].reshape(subs, unit, HD)

    everything = frozenset(range(len(labels)))
    if first:

        @pl.when(furthest + span <= clear)
        def _():
            work(frozenset())

        @pl.when(furthest + span > clear)
        def _():
            work(everything)
    elif last:
        work(everything)
    else:
        jobs = lax.axis_size("ctx") // members
        second_half = job >= jobs // 2
        near = frozenset(p for p, (k, _) in enumerate(labels) if k < jobs // 2)

        @pl.when(second_half)
        def _():
            work(near)

        @pl.when(jnp.logical_not(second_half))
        def _():
            work(everything - near)


def attend(part, bounds, queries, kvs, labels, states, last, count, members, sets, subs, local_kv):
    rows = queries[0].shape[0] // PARTS
    unit = rows * GROUPS
    total = len(sets) * subs * unit
    span = kvs[0].shape[1]
    in_specs = [pl.BlockSpec((subs * rows, COLS), lambda t, part, _: (part[0] // subs + t, 0))] * len(sets)
    in_specs += [pl.BlockSpec(k.shape, lambda t, *_: (0, 0, 0)) for k in kvs]
    kept = pl.BlockSpec((subs, unit, 2 * HD), lambda t, part, _: (part[0] // subs + t, 0, 0))
    args = list(queries) + list(kvs)
    if states is not None:
        in_specs += [kept] * len(sets)
        args += list(states)
    if last:
        out_shape = jax.ShapeDtypeStruct((len(sets), rows, COLS), jnp.bfloat16)
        out_spec = pl.BlockSpec((len(sets), rows, COLS), lambda t, *_: (0, 0, 0))
    else:
        out_shape = [jax.ShapeDtypeStruct((count * subs, unit, 2 * HD), jnp.float32)] * len(sets)
        out_spec = [kept] * len(sets)
    width = min(1024, span)
    positions = span * len(kvs)
    return pl.pallas_call(
        functools.partial(
            attend_kernel,
            labels=labels,
            sets=tuple(sets),
            subs=subs,
            first=states is None,
            last=last,
            width=width,
            rows=rows,
            members=members,
            local_kv=local_kv,
        ),
        out_shape=out_shape,
        grid_spec=pltpu.PrefetchScalarGridSpec(
            num_scalar_prefetch=2,
            grid=(count,),
            in_specs=in_specs,
            out_specs=out_spec,
            scratch_shapes=[pltpu.VMEM((total, width), jnp.float32)] * 2 + [pltpu.VMEM((total, HD), jnp.int32)],
        ),
        cost_estimate=pl.CostEstimate(
            flops=count * total * positions * HD * 10,
            bytes_accessed=positions * HD * 4 + count * total * HD * 4,
            transcendentals=count * total * positions,
        ),
        compiler_params=pltpu.CompilerParams(vmem_limit_bytes=VMEM_LIMIT),
    )(jnp.full((1,), part, jnp.int32), bounds, *args)


def project_kernel(*refs, members, local_kv, size, devices):
    ins, (w_ref, keep_ref, send_ref, lhs) = refs[:members], refs[members:]

    @pl.when(pl.program_id(0) == 0)
    def _():
        position, here = lax.axis_index("ctx"), lax.axis_index("heads")
        job, member = lax.div(position, members), lax.rem(position, members)
        share = devices // size
        for m, ref in enumerate(ins):
            for k in range(ref.shape[0]):
                source = lax.bitwise_xor(job, k)
                column = lax.rem(source, local_kv)
                for s in range(local_kv):
                    row_set = lax.bitwise_xor(s, column)
                    owner = (source - column + row_set) * members + lax.bitwise_xor(member, m)
                    away, slot = lax.bitwise_xor(lax.div(owner, share), here), 0
                    bits = size.bit_length() - 1
                    for b in range(bits):
                        slot = slot + lax.rem(lax.div(away, 2**b), 2) * 2 ** (bits - 1 - b)
                    lhs[column, slot * share + lax.rem(owner, share)] = ref[k, s]

    rows, cols = lhs.shape[1] * lhs.shape[2], lhs.shape[3]
    acc = None
    for c in range(lhs.shape[0]):
        left = lhs[c].reshape(rows, cols)
        term = jnp.dot(left, w_ref[c * cols : (c + 1) * cols, :], preferred_element_type=jnp.float32)
        acc = term if acc is None else acc + term
    keep_ref[...] = acc[: rows // 2].astype(keep_ref.dtype)
    send_ref[...] = acc[rows // 2 :].astype(send_ref.dtype)


def project(pieces, weight, devices, size, cut, cuts):
    jobs, sets, rows, cols = pieces[0].shape
    depth, out_cols = weight.shape
    out_cols = out_cols // cuts
    width = min(512, out_cols)
    steps = out_cols // width
    total = devices * rows
    half = jax.ShapeDtypeStruct((total // 2, out_cols), jnp.bfloat16)
    return pl.pallas_call(
        functools.partial(
            project_kernel, members=len(pieces), local_kv=sets, size=size, devices=devices
        ),
        out_shape=(half, half),
        grid=(out_cols // width,),
        in_specs=[pl.BlockSpec(p.shape, lambda t: (0, 0, 0, 0)) for p in pieces]
        + [pl.BlockSpec((depth, width), lambda t: (0, cut * steps + t))],
        out_specs=(pl.BlockSpec((total // 2, width), lambda t: (0, t)),) * 2,
        scratch_shapes=[pltpu.VMEM((sets, devices, rows, cols), jnp.bfloat16)],
        cost_estimate=pl.CostEstimate(
            flops=2 * total * depth * out_cols,
            bytes_accessed=2 * (depth * out_cols + total * out_cols + total * depth),
            transcendentals=0,
        ),
        compiler_params=pltpu.CompilerParams(vmem_limit_bytes=VMEM_LIMIT),
    )(*pieces, weight)


def crossed(block, bits, axis="ctx"):
    return lax.ppermute(block, axis, [(i, i ^ bits) for i in range(lax.axis_size(axis))])


def after(block, *others):
    return lax.optimization_barrier((block,) + others)[0]


def shards(queries, cache_keys, cache_values, bounds, out_weight, residual):
    rows = queries.shape[0]
    prompts = cache_keys.shape[0]
    local_kv = cache_keys.shape[2] // HD
    devices, size = lax.axis_size("ctx"), lax.axis_size("heads")
    jobs = prompts * local_kv
    members = devices // jobs
    every = range(1, members)
    final = jobs - 1
    middle = list(range(jobs - 2, 0, -1))
    kvs_of = list(range(local_kv))

    ready = pack(queries, cache_keys, cache_values, middle[:1] + [0], kvs_of, members, local_kv)
    slabs = dict(zip(middle[:1] + [0], ready, strict=False))
    queries_of = ready[len(slabs) :]
    rest = middle[1:] + [final]
    slabs.update(zip(rest, pack(after(queries, ready[0]), cache_keys, cache_values, rest, [], members, local_kv), strict=True))

    query = [queries_of[0]] + [crossed(queries_of[k], k * members) for k in range(1, local_kv)]
    got = {(0, 0): slabs[0]}
    for k in middle + [final]:
        got[k, 0] = crossed(slabs[k], k * members)
    for m in every:
        got[0, m] = crossed(got[0, 0], m)
    labels = [(0, m) for m in range(members)]
    everyone = list(range(local_kv))
    slabs = [got[i] for i in labels]
    state = []
    for k in everyone:
        q = after(query[k], *state) if state else query[k]
        state += attend(0, bounds, [q], slabs, labels, None, False, PARTS // 2, members, [k], 2, local_kv)
    if middle:
        direct = [(k, 0) for k in middle]
        for i in direct:
            got[i] = after(got[i], state)
        for k in middle:
            for m in every:
                got[k, m] = crossed(got[k, 0], m)
        if len(direct) > 1:
            got[direct[-1]] = after(got[direct[-1]], *[got[middle[0], m] for m in every])
        slabs = [got[i] for i in direct]
        state = attend(0, bounds, query, slabs, direct, state, False, PARTS, members, everyone, 1, local_kv)
    got[final, 0] = after(got[final, 0], state)
    for m in every:
        got[final, m] = crossed(got[final, 0], m)
    labels = [(k, m) for k in middle for m in every] + [(final, m) for m in range(members)]

    step = rows // PARTS
    blocks = residual.reshape(devices // size, rows, residual.shape[1])
    pieces, packs, partials, sums, outs = {}, {}, {}, {}, {}

    def late(part, *waits):
        q = [after(query[0], *waits)] + query[1:] if waits else query
        slabs = [got[i] for i in labels]
        pieces[part] = attend(part, bounds, q, slabs, labels, state, True, 1, members, everyone, 1, local_kv)

    def gathered(part, *waits):
        received = [crossed(pieces[part], k * members) for k in range(1, jobs)]
        received = list(after(tuple(received), *waits))
        own = jnp.stack([pieces[part]] + received)
        packs[part] = [own] + [crossed(own, m) for m in every]

    def projected(part, cut, cuts, *waits):
        own = after(packs[part][0], *waits) if waits else packs[part][0]
        partials[part, cut] = project([own] + packs[part][1:], out_weight, devices, size, cut, cuts)

    def sent(key, level):
        return crossed((partials[key] if level == 0 else sums[key])[1], 2**level, "heads")

    def combined(key, level, block):
        keep = (partials[key] if level == 0 else sums[key])[0].astype(jnp.float32)
        block = block.astype(jnp.float32)
        if 2 ** (level + 1) < size:
            half = keep.shape[0] // 2
            sums[key] = keep[:half] + block[:half], (keep[half:] + block[half:]).astype(jnp.bfloat16)
        else:
            part, cut = key
            cols = keep.shape[1]
            res = blocks[:, part * step : (part + 1) * step, cut * cols : (cut + 1) * cols].reshape(-1, cols)
            total = res.astype(jnp.float32) + (keep + block)
            outs[key] = total.astype(jnp.bfloat16).reshape(devices // size, step, cols)

    levels = size.bit_length() - 1
    for turn in range(PARTS):
        waits = [pieces[turn - 1]] if turn >= 1 else []
        if turn >= 2:
            waits.append(partials[turn - 2, 0][0])
        late(turn, *waits)
        here = [((turn - 2 - level, 0), level) for level in range(levels) if turn - 2 - level >= 0]
        received = [sent(key, level) for key, level in here]
        if received:
            received, pieces[turn] = after((received, pieces[turn]))
        for (key, level), block in zip(here, received, strict=True):
            combined(key, level, block)
        if turn >= 1:
            gathered(turn - 1, pieces[turn])
            projected(turn - 1, 0, 1, *([sums[turn - 2, 0][1]] if (turn - 2, 0) in sums else []))
    final = PARTS - 1
    older = [((PARTS - 2 - level, 0), level) for level in range(1, levels) if PARTS - 2 - level >= 0]
    received = [sent(key, level) for key, level in older]
    gathered(final, partials[final - 1, 0][0], *received)
    for (key, level), block in zip(older, received, strict=True):
        combined(key, level, block)
    doing = [((PARTS - 2, 0), 0)]
    received = [sent(*doing[0])]
    projected(final, 0, CUTS)
    for cut in range(1, CUTS):
        doing += [((final, cut - 1), 0)]
        received += [sent((final, cut - 1), 0)]
        projected(final, cut, CUTS, partials[final, cut - 1][0])
    partials[final, CUTS - 1], received = after((partials[final, CUTS - 1], received))
    for (key, level), block in zip(doing, received, strict=True):
        combined(key, level, block)
    doing = [(key, level + 1) for key, level in older + doing if level + 1 < levels] + [((final, CUTS - 1), 0)]
    ends = []
    while doing:
        received = [sent(key, level) for key, level in doing]
        for (key, level), block in zip(doing, received, strict=True):
            if level + 1 < levels:
                combined(key, level, block)
            else:
                ends.append((key, level, block))
        doing = [(key, level + 1) for key, level in doing if level + 1 < levels]
    received = after([block for _, _, block in ends])
    for (key, level, _), block in zip(ends, received, strict=True):
        combined(key, level, block)
    last = jnp.concatenate([outs[final, c] for c in range(CUTS)], axis=2)
    return jnp.concatenate([outs[p, 0] for p in range(final)] + [last], axis=1).reshape(residual.shape)


def solution(mesh):
    in_specs = (
        P("ctx", "heads"),
        P(None, "ctx", "heads"),
        P(None, "ctx", "heads"),
        P(),
        P("heads", "ctx"),
        P("heads", "ctx"),
    )
    out_specs = P("heads", "ctx")
    return jax.shard_map(shards, mesh=mesh, in_specs=in_specs, out_specs=out_specs, check_vma=False)
```

```python
import functools
import math

import jax
import jax.numpy as jnp
from jax import lax
from jax.experimental import pallas as pl
from jax.experimental.pallas import tpu as pltpu
from jax.sharding import PartitionSpec as P

HD = 128
GROUPS = 16
COLS = GROUPS * HD
NEG_FILL = -1e30
PARTS = 4
CUTS = 2
VMEM_LIMIT = 50 * 2**20


def pack_kernel(q_ref, k_ref, v_ref, *refs, jobs_of, kvs_of, members, local_kv):
    outs, sems = refs[:-1], refs[-1]
    job = lax.div(lax.axis_index("ctx"), members)
    copies = []
    for out, k in zip(outs, jobs_of, strict=False):
        other = lax.bitwise_xor(job, k)
        prompt, place = lax.div(other, local_kv), lax.rem(other, local_kv)
        for i, ref in enumerate((k_ref, v_ref)):
            copies.append((ref.at[prompt, :, pl.ds(pl.multiple_of(place * HD, HD), HD)], out.at[i]))
    for out, k in zip(outs[len(jobs_of) :], kvs_of, strict=True):
        place = lax.rem(lax.bitwise_xor(job, k), local_kv)
        copies.append((q_ref.at[:, pl.ds(pl.multiple_of(place * COLS, COLS), COLS)], out))
    copies = [pltpu.make_async_copy(a, b, sems.at[n]) for n, (a, b) in enumerate(copies)]
    for c in copies:
        c.start()
    for c in copies:
        c.wait()


def pack(queries, keys, values, jobs_of, kvs_of, members, local_kv):
    slab = jax.ShapeDtypeStruct((2, keys.shape[1], HD), keys.dtype)
    cut = jax.ShapeDtypeStruct((queries.shape[0], COLS), queries.dtype)
    anywhere = pl.BlockSpec(memory_space=pl.ANY)
    outs = [slab] * len(jobs_of) + [cut] * len(kvs_of)
    return pl.pallas_call(
        functools.partial(pack_kernel, jobs_of=jobs_of, kvs_of=kvs_of, members=members, local_kv=local_kv),
        out_shape=outs,
        in_specs=[anywhere] * 3,
        out_specs=[pl.BlockSpec(memory_space=pltpu.VMEM)] * len(outs),
        scratch_shapes=[pltpu.SemaphoreType.DMA((2 * len(jobs_of) + len(kvs_of),))],
        compiler_params=pltpu.CompilerParams(vmem_limit_bytes=VMEM_LIMIT),
        cost_estimate=pl.CostEstimate(flops=0, bytes_accessed=sum(2 * 2 * math.prod(o.shape) for o in outs), transcendentals=0),
    )(queries, keys, values)


def attend_kernel(part_ref, bounds_ref, *refs, labels, sets, subs, first, last, width, rows, members, local_kv):
    queries, kvs = refs[: len(sets)], refs[len(sets) : len(sets) + len(labels)]
    refs = refs[len(sets) + len(labels) :]
    if not first:
        states_in, refs = refs[: len(sets)], refs[len(sets) :]
    outs, (buf_a, buf_b, lim_ref) = refs[:-3], refs[-3:]
    bufs = (buf_a, buf_b)
    position = lax.axis_index("ctx")
    job, member = lax.div(position, members), lax.rem(position, members)
    prompt, place = lax.div(job, local_kv), lax.rem(job, local_kv)
    start, length = bounds_ref[prompt, 0], bounds_ref[prompt, 1]
    part = part_ref[0] + pl.program_id(0) * subs
    unit = rows * GROUPS
    total = len(sets) * subs * unit
    span = kvs[0].shape[1]
    bases = [(lax.bitwise_xor(job, k) * members + lax.bitwise_xor(member, m)) * span for k, m in labels]
    blocks = [(p, j) for p in range(len(labels)) for j in range(span // width)]

    query = jnp.concatenate([q[...] for q in queries], axis=0).astype(jnp.float32)
    query = query * (math.log2(math.e) / math.sqrt(HD))
    high = query.astype(jnp.bfloat16)
    low = (query - high.astype(jnp.float32)).astype(jnp.bfloat16)

    def stacked(t):
        parts = range(0, len(sets) * subs * rows, rows)
        return jnp.concatenate([t[n : n + rows, h * HD : (h + 1) * HD] for n in parts for h in range(GROUPS)], axis=0)

    query = jnp.concatenate([stacked(high), stacked(low)], axis=1)
    clear = jnp.minimum(start + 1, length)
    furthest = bases[0]
    for b in bases[1:]:
        furthest = jnp.maximum(furthest, b)

    def set_limits():
        index = lax.broadcasted_iota(jnp.int32, (total, HD), 0)
        which = lax.div(index, unit)
        row_set = lax.bitwise_xor(lax.div(which, subs) + sets[0], place)
        row = (part + lax.rem(which, subs)) * rows + lax.rem(index, rows)
        row = row + (row_set * members + member) * (rows * PARTS)
        lim_ref[...] = jnp.minimum(start + row + 1, length)

    def score(block, s_ref, running, masked):
        p, j = block
        masked = p in masked
        keys = kvs[p][0, j * width : (j + 1) * width, :]
        s = lax.dot_general(
            query,
            jnp.concatenate([keys, keys], axis=1),
            (((1,), (1,)), ((), ())),
            preferred_element_type=jnp.float32,
        )
        if masked:
            limit = jnp.concatenate([lim_ref[...] - (bases[p] + j * width)] * (width // HD), axis=1)
            s = jnp.where(lax.broadcasted_iota(jnp.int32, s.shape, 1) < limit, s, NEG_FILL)
        s_ref[...] = s
        return jnp.maximum(running, jnp.max(s, axis=1, keepdims=True))

    def mix(block, s_ref, before, now, acc):
        p, j = block
        values = kvs[p][1, j * width : (j + 1) * width, :]
        values = jnp.concatenate([values, jnp.ones_like(values)], axis=1)
        weights = jnp.exp2(s_ref[...] - now).astype(jnp.bfloat16)
        new = jnp.dot(weights, values, preferred_element_type=jnp.float32)
        return new if acc is None else acc * jnp.exp2(before - now) + new

    def work(masked):
        if masked:
            set_limits()
        if first:
            before, acc = jnp.full((total, 1), NEG_FILL, jnp.float32), None
        else:
            kept = jnp.concatenate([t[...].reshape(subs * unit, 2 * HD) for t in states_in], axis=0)
            before = kept[:, HD : HD + 1]
            acc = jnp.concatenate([kept[:, :HD], jnp.broadcast_to(kept[:, 2 * HD - 1 :], (total, HD))], axis=1)
        now = score(blocks[0], bufs[0], before, masked)
        for n, block in enumerate(blocks):
            more = n + 1 < len(blocks)
            if more:
                after = score(blocks[n + 1], bufs[(n + 1) % 2], now, masked)
            acc = mix(block, bufs[n % 2], before, now, acc)
            if more:
                before, now = now, after
        if last:
            out = (acc[:, :HD] / acc[:, HD:]).astype(outs[0].dtype)
            for n in range(len(sets)):
                for h in range(GROUPS):
                    begin = n * unit + h * rows
                    outs[0][n, :, h * HD : (h + 1) * HD] = out[begin : begin + rows]
        else:
            lane = lax.broadcasted_iota(jnp.int32, (total, HD), 1)
            stats = jnp.where(lane < HD // 2, jnp.broadcast_to(now, (total, HD)), acc[:, HD:])
            for n, out_ref in enumerate(outs):
                rest = slice(n * subs * unit, (n + 1) * subs * unit)
                out_ref[:, :, :HD] = acc[rest, :HD].reshape(subs, unit, HD)
                out_ref[:, :, HD:] = stats[rest].reshape(subs, unit, HD)

    everything = frozenset(range(len(labels)))
    if first:

        @pl.when(furthest + span <= clear)
        def _():
            work(frozenset())

        @pl.when(furthest + span > clear)
        def _():
            work(everything)
    elif last:
        work(everything)
    else:
        jobs = lax.axis_size("ctx") // members
        second_half = job >= jobs // 2
        near = frozenset(p for p, (k, _) in enumerate(labels) if k < jobs // 2)

        @pl.when(second_half)
        def _():
            work(near)

        @pl.when(jnp.logical_not(second_half))
        def _():
            work(everything - near)


def attend(part, bounds, queries, kvs, labels, states, last, count, members, sets, subs, local_kv):
    rows = queries[0].shape[0] // PARTS
    unit = rows * GROUPS
    total = len(sets) * subs * unit
    span = kvs[0].shape[1]
    in_specs = [pl.BlockSpec((subs * rows, COLS), lambda t, part, _: (part[0] // subs + t, 0))] * len(sets)
    in_specs += [pl.BlockSpec(k.shape, lambda t, *_: (0, 0, 0)) for k in kvs]
    kept = pl.BlockSpec((subs, unit, 2 * HD), lambda t, part, _: (part[0] // subs + t, 0, 0))
    args = list(queries) + list(kvs)
    if states is not None:
        in_specs += [kept] * len(sets)
        args += list(states)
    if last:
        out_shape = jax.ShapeDtypeStruct((len(sets), rows, COLS), jnp.bfloat16)
        out_spec = pl.BlockSpec((len(sets), rows, COLS), lambda t, *_: (0, 0, 0))
    else:
        out_shape = [jax.ShapeDtypeStruct((count * subs, unit, 2 * HD), jnp.float32)] * len(sets)
        out_spec = [kept] * len(sets)
    width = min(1024, span)
    positions = span * len(kvs)
    return pl.pallas_call(
        functools.partial(
            attend_kernel,
            labels=labels,
            sets=tuple(sets),
            subs=subs,
            first=states is None,
            last=last,
            width=width,
            rows=rows,
            members=members,
            local_kv=local_kv,
        ),
        out_shape=out_shape,
        grid_spec=pltpu.PrefetchScalarGridSpec(
            num_scalar_prefetch=2,
            grid=(count,),
            in_specs=in_specs,
            out_specs=out_spec,
            scratch_shapes=[pltpu.VMEM((total, width), jnp.float32)] * 2 + [pltpu.VMEM((total, HD), jnp.int32)],
        ),
        cost_estimate=pl.CostEstimate(
            flops=count * total * positions * HD * 10,
            bytes_accessed=positions * HD * 4 + count * total * HD * 4,
            transcendentals=count * total * positions,
        ),
        compiler_params=pltpu.CompilerParams(vmem_limit_bytes=VMEM_LIMIT),
    )(jnp.full((1,), part, jnp.int32), bounds, *args)


def project_kernel(*refs, members, local_kv, size, devices):
    ins, (w_ref, keep_ref, send_ref, lhs) = refs[:members], refs[members:]

    @pl.when(pl.program_id(0) == 0)
    def _():
        position, here = lax.axis_index("ctx"), lax.axis_index("heads")
        job, member = lax.div(position, members), lax.rem(position, members)
        share = devices // size
        for m, ref in enumerate(ins):
            for k in range(ref.shape[0]):
                source = lax.bitwise_xor(job, k)
                column = lax.rem(source, local_kv)
                for s in range(local_kv):
                    row_set = lax.bitwise_xor(s, column)
                    owner = (source - column + row_set) * members + lax.bitwise_xor(member, m)
                    away, slot = lax.bitwise_xor(lax.div(owner, share), here), 0
                    bits = size.bit_length() - 1
                    for b in range(bits):
                        slot = slot + lax.rem(lax.div(away, 2**b), 2) * 2 ** (bits - 1 - b)
                    lhs[column, slot * share + lax.rem(owner, share)] = ref[k, s]

    rows, cols = lhs.shape[1] * lhs.shape[2], lhs.shape[3]
    acc = None
    for c in range(lhs.shape[0]):
        left = lhs[c].reshape(rows, cols)
        term = jnp.dot(left, w_ref[c * cols : (c + 1) * cols, :], preferred_element_type=jnp.float32)
        acc = term if acc is None else acc + term
    keep_ref[...] = acc[: rows // 2].astype(keep_ref.dtype)
    send_ref[...] = acc[rows // 2 :].astype(send_ref.dtype)


def project(pieces, weight, devices, size, cut, cuts):
    jobs, sets, rows, cols = pieces[0].shape
    depth, out_cols = weight.shape
    out_cols = out_cols // cuts
    width = min(512, out_cols)
    steps = out_cols // width
    total = devices * rows
    half = jax.ShapeDtypeStruct((total // 2, out_cols), jnp.bfloat16)
    return pl.pallas_call(
        functools.partial(
            project_kernel, members=len(pieces), local_kv=sets, size=size, devices=devices
        ),
        out_shape=(half, half),
        grid=(out_cols // width,),
        in_specs=[pl.BlockSpec(p.shape, lambda t: (0, 0, 0, 0)) for p in pieces]
        + [pl.BlockSpec((depth, width), lambda t: (0, cut * steps + t))],
        out_specs=(pl.BlockSpec((total // 2, width), lambda t: (0, t)),) * 2,
        scratch_shapes=[pltpu.VMEM((sets, devices, rows, cols), jnp.bfloat16)],
        cost_estimate=pl.CostEstimate(
            flops=2 * total * depth * out_cols,
            bytes_accessed=2 * (depth * out_cols + total * out_cols + total * depth),
            transcendentals=0,
        ),
        compiler_params=pltpu.CompilerParams(vmem_limit_bytes=VMEM_LIMIT),
    )(*pieces, weight)


def crossed(block, bits, axis="ctx"):
    return lax.ppermute(block, axis, [(i, i ^ bits) for i in range(lax.axis_size(axis))])


def after(block, *others):
    return lax.optimization_barrier((block,) + others)[0]


def shards(queries, cache_keys, cache_values, bounds, out_weight, residual):
    rows = queries.shape[0]
    prompts = cache_keys.shape[0]
    local_kv = cache_keys.shape[2] // HD
    devices, size = lax.axis_size("ctx"), lax.axis_size("heads")
    jobs = prompts * local_kv
    members = devices // jobs
    every = range(1, members)
    final = jobs - 1
    middle = list(range(jobs - 2, 0, -1))
    kvs_of = list(range(local_kv))

    ready = pack(queries, cache_keys, cache_values, middle[:1] + [0], kvs_of, members, local_kv)
    slabs = dict(zip(middle[:1] + [0], ready, strict=False))
    queries_of = ready[len(slabs) :]
    rest = middle[1:] + [final]
    slabs.update(zip(rest, pack(after(queries, ready[0]), cache_keys, cache_values, rest, [], members, local_kv), strict=True))

    query = [queries_of[0]] + [crossed(queries_of[k], k * members) for k in range(1, local_kv)]
    got = {(0, 0): slabs[0]}
    for k in middle + [final]:
        got[k, 0] = crossed(slabs[k], k * members)
    for m in every:
        got[0, m] = crossed(got[0, 0], m)
    labels = [(0, m) for m in range(members)]
    everyone = list(range(local_kv))
    slabs = [got[i] for i in labels]
    state = []
    for k in everyone:
        q = after(query[k], *state) if state else query[k]
        state += attend(0, bounds, [q], slabs, labels, None, False, PARTS // 2, members, [k], 2, local_kv)
    if middle:
        direct = [(k, 0) for k in middle]
        for i in direct:
            got[i] = after(got[i], state)
        for k in middle:
            for m in every:
                got[k, m] = crossed(got[k, 0], m)
        if len(direct) > 1:
            got[direct[-1]] = after(got[direct[-1]], *[got[middle[0], m] for m in every])
        slabs = [got[i] for i in direct]
        state = attend(0, bounds, query, slabs, direct, state, False, PARTS, members, everyone, 1, local_kv)
    got[final, 0] = after(got[final, 0], state)
    for m in every:
        got[final, m] = crossed(got[final, 0], m)
    labels = [(k, m) for k in middle for m in every] + [(final, m) for m in range(members)]

    step = rows // PARTS
    blocks = residual.reshape(devices // size, rows, residual.shape[1])
    pieces, packs, partials, sums, outs = {}, {}, {}, {}, {}

    def late(part, *waits):
        q = [after(query[0], *waits)] + query[1:] if waits else query
        slabs = [got[i] for i in labels]
        pieces[part] = attend(part, bounds, q, slabs, labels, state, True, 1, members, everyone, 1, local_kv)

    def gathered(part, *waits):
        received = [crossed(pieces[part], k * members) for k in range(1, jobs)]
        received = list(after(tuple(received), *waits))
        own = jnp.stack([pieces[part]] + received)
        packs[part] = [own] + [crossed(own, m) for m in every]

    def projected(part, cut, cuts, *waits):
        own = after(packs[part][0], *waits) if waits else packs[part][0]
        partials[part, cut] = project([own] + packs[part][1:], out_weight, devices, size, cut, cuts)

    def sent(key, level):
        return crossed((partials[key] if level == 0 else sums[key])[1], 2**level, "heads")

    def combined(key, level, block):
        keep = (partials[key] if level == 0 else sums[key])[0].astype(jnp.float32)
        block = block.astype(jnp.float32)
        if 2 ** (level + 1) < size:
            half = keep.shape[0] // 2
            sums[key] = keep[:half] + block[:half], (keep[half:] + block[half:]).astype(jnp.bfloat16)
        else:
            part, cut = key
            cols = keep.shape[1]
            res = blocks[:, part * step : (part + 1) * step, cut * cols : (cut + 1) * cols].reshape(-1, cols)
            total = res.astype(jnp.float32) + (keep + block)
            outs[key] = total.astype(jnp.bfloat16).reshape(devices // size, step, cols)

    levels = size.bit_length() - 1
    for turn in range(PARTS):
        waits = [pieces[turn - 1]] if turn >= 1 else []
        if turn >= 2:
            waits.append(partials[turn - 2, 0][0])
        late(turn, *waits)
        here = [((turn - 2 - level, 0), level) for level in range(levels) if turn - 2 - level >= 0]
        received = [sent(key, level) for key, level in here]
        if received:
            received, pieces[turn] = after((received, pieces[turn]))
        for (key, level), block in zip(here, received, strict=True):
            combined(key, level, block)
        if turn >= 1:
            gathered(turn - 1, pieces[turn])
            projected(turn - 1, 0, 1, *([sums[turn - 2, 0][1]] if (turn - 2, 0) in sums else []))
    final = PARTS - 1
    older = [((PARTS - 2 - level, 0), level) for level in range(1, levels) if PARTS - 2 - level >= 0]
    received = [sent(key, level) for key, level in older]
    gathered(final, partials[final - 1, 0][0], *received)
    for (key, level), block in zip(older, received, strict=True):
        combined(key, level, block)
    doing = [((PARTS - 2, 0), 0)]
    received = [sent(*doing[0])]
    projected(final, 0, CUTS)
    for cut in range(1, CUTS):
        doing += [((final, cut - 1), 0)]
        received += [sent((final, cut - 1), 0)]
        projected(final, cut, CUTS, partials[final, cut - 1][0])
    received = [after(block, partials[final, CUTS - 1][0]) for block in received]
    for (key, level), block in zip(doing, received, strict=True):
        combined(key, level, block)
    doing = [(key, level + 1) for key, level in older + doing if level + 1 < levels] + [((final, CUTS - 1), 0)]
    ends = []
    while doing:
        received = [sent(key, level) for key, level in doing]
        for (key, level), block in zip(doing, received, strict=True):
            if level + 1 < levels:
                combined(key, level, block)
            else:
                ends.append((key, level, block))
        doing = [(key, level + 1) for key, level in doing if level + 1 < levels]
    received = after([block for _, _, block in ends])
    for (key, level, _), block in zip(ends, received, strict=True):
        combined(key, level, block)
    last = jnp.concatenate([outs[final, c] for c in range(CUTS)], axis=2)
    return jnp.concatenate([outs[p, 0] for p in range(final)] + [last], axis=1).reshape(residual.shape)


def solution(mesh):
    in_specs = (
        P("ctx", "heads"),
        P(None, "ctx", "heads"),
        P(None, "ctx", "heads"),
        P(),
        P("heads", "ctx"),
        P("heads", "ctx"),
    )
    out_specs = P("heads", "ctx")
    return jax.shard_map(shards, mesh=mesh, in_specs=in_specs, out_specs=out_specs, check_vma=False)
```
